32 devices in a mesh: parts: 2 (over x), row: 4 (over y, core), col: 4 (over z).
Axes of the slice: x: 2, y: 2, z: 4, core: 2. Of those that a mesh axis runs over, the one named last changes fastest.
Arguments:
- pair: bfloat16 [192, 96, 128], P(('parts', 'row'), 'col'), parts along dimension 0, may hold values from -6 to 6
- residue_count: int32 [2], P('parts'), parts along dimension 0, may hold values from 48 to 96
- out_norm: float32 [128], replicated, may hold values from 0.1 to 1.9
- out_proj: bfloat16 [128, 512], replicated, may hold values from -0.5 to 0.5
- out_gate: bfloat16 [128, 128], replicated, may hold values from -0.5 to 0.5
- out_mix_norm: float32 [128], replicated, may hold values from 0.1 to 1.9
- out_final: bfloat16 [128, 128], replicated, may hold values from -0.5 to 0.5
- inc_norm: float32 [128], replicated, may hold values from 0.1 to 1.9
- inc_proj: bfloat16 [128, 512], replicated, may hold values from -0.5 to 0.5
- inc_gate: bfloat16 [128, 128], replicated, may hold values from -0.5 to 0.5
- inc_mix_norm: float32 [128], replicated, may hold values from 0.1 to 1.9
- inc_final: bfloat16 [128, 128], replicated, may hold values from -0.5 to 0.5
- transition_norm: float32 [128], replicated, may hold values from 0.1 to 1.9
- transition_up: bfloat16 [128, 1024], replicated, may hold values from -0.5 to 0.5
- transition_down: bfloat16 [512, 128], replicated, may hold values from -0.25 to 0.25
Outputs:
- result: bfloat16 [192, 96, 128], P(('parts', 'row'), 'col'), parts along dimension 0
The draws below stay inside these ranges and needn't reach their ends.
There are 2 independent parts, one for each index of `parts`. The reference program is written for one: setup_inputs(seed, part) draws one part's arguments, and reference() takes and returns one part's arrays. A program takes and returns all parts, laid end to end along the dimension named above; an argument that names none is the same for every part. Nothing has to cross between parts.
Inputs may be any that keep to these rules, and one draw needn't show every extreme that they name: `residue_count`: how many residues of the complex are real; positions below it are real, the others padding.
All inputs are finite; a program needn't handle non-finite values.
Results may differ from the reference program's by a relative error of at most 0.015.
Values may be sent and summed in bfloat16 or wider, within the bound.
A program may use at most 128 MiB of HBM per device.

```python
import jax
import jax.numpy as jnp
from jax import lax

C = 128
H = 128
TRANS = 512
N = 96
N_ROW = 4


def level_of(own_key, extent, shards, least, largest):
    def one(position, blocks):
        heights = jax.random.uniform(jax.random.fold_in(jax.random.fold_in(own_key, 6), position), (blocks,), jnp.float32, least / len(shards), largest / len(shards))
        return jnp.repeat(jnp.exp(heights), extent[position] // blocks).reshape((-1,) + (1,) * (len(extent) - position - 1))

    loudness = one(*shards[0])
    for cut in shards[1:]:
        loudness = loudness * one(*cut)
    return loudness


def gaussian(rng, shape, scale, bound, shards=(), held_as=jnp.bfloat16):
    values = jax.random.normal(rng, shape, jnp.float32) * scale
    if len(shards) > 0:
        values = level_of(rng, shape, shards, -0.22, 0.18) * values
    return jnp.clip(values, min=-bound, max=bound).astype(held_as)


def setup_inputs(seed: int = 0, part: int = 0) -> dict:
    key_list = jax.random.split(jax.random.key(seed), 16)
    part_keys = jax.random.split(jax.random.fold_in(key_list[15], part), 16)
    return {
        "pair": gaussian(part_keys[0], (N, N, C), 1.0, 6.0, ((0, 4), (1, 4))),
        "residue_count": jax.random.randint(part_keys[1], (1,), N // 2, N + 1).astype(jnp.int32),
        "out_norm": jnp.clip(1.0 + 0.18 * jax.random.normal(key_list[2], (C,), jnp.float32), 0.1, 1.9),
        "out_proj": gaussian(key_list[3], (C, 4 * H), C ** -0.5, 0.5),
        "out_gate": gaussian(key_list[4], (C, C), C ** -0.5, 0.5),
        "out_mix_norm": jnp.clip(1.0 + 0.18 * jax.random.normal(key_list[5], (H,), jnp.float32), 0.1, 1.9),
        "out_final": gaussian(key_list[6], (H, C), H ** -0.5, 0.5),
        "inc_norm": jnp.clip(1.0 + 0.18 * jax.random.normal(key_list[7], (C,), jnp.float32), 0.1, 1.9),
        "inc_proj": gaussian(key_list[8], (C, 4 * H), C ** -0.5, 0.5),
        "inc_gate": gaussian(key_list[9], (C, C), C ** -0.5, 0.5),
        "inc_mix_norm": jnp.clip(1.0 + 0.18 * jax.random.normal(key_list[10], (H,), jnp.float32), 0.1, 1.9),
        "inc_final": gaussian(key_list[11], (H, C), H ** -0.5, 0.5),
        "transition_norm": jnp.clip(1.0 + 0.18 * jax.random.normal(key_list[12], (C,), jnp.float32), 0.1, 1.9),
        "transition_up": gaussian(key_list[13], (C, 2 * TRANS), C ** -0.5, 0.5),
        "transition_down": gaussian(key_list[14], (TRANS, C), TRANS ** -0.5, 0.25),
    }


def layer_norm(values, gain):
    mean = lax.optimization_barrier(jnp.mean(values, axis=-1, keepdims=True))
    centred = values - mean
    spread = lax.optimization_barrier(jnp.mean(centred * centred, axis=-1, keepdims=True))
    return centred * lax.rsqrt(spread + 1e-05) * gain.astype(jnp.float32)

def reference(pair, residue_count, out_norm, out_proj, out_gate, out_mix_norm, out_final, inc_norm, inc_proj, inc_gate, inc_mix_norm, inc_final, transition_norm, transition_up, transition_down):
    rows = N // N_ROW
    valid = (jnp.arange(N, dtype=jnp.int32) < residue_count[0]).astype(jnp.float32)

    def update(current, norm_gain, proj_w, gate_w, mix_gain, final_w, incoming):
        hidden = proj_w.shape[1] // 4

        def project(block):
            start = (block * rows).astype(jnp.int32)
            piece = lax.dynamic_slice_in_dim(current, start, rows, 0)
            normed = layer_norm(piece.astype(jnp.float32), norm_gain).astype(jnp.bfloat16)
            part = jnp.dot(normed, proj_w, preferred_element_type=jnp.float32)
            row_mask = lax.dynamic_slice_in_dim(valid, start, rows, 0)
            mask = row_mask[:, None, None] * valid[None, :, None]
            left = (mask * jax.nn.sigmoid(part[..., :hidden]) * part[..., hidden:2 * hidden]).astype(jnp.bfloat16)
            right = (mask * jax.nn.sigmoid(part[..., 2 * hidden:3 * hidden]) * part[..., 3 * hidden:]).astype(jnp.bfloat16)
            gate = jnp.dot(normed, gate_w, preferred_element_type=jnp.float32)
            return (left, right, gate)
        left, right, gate = lax.map(project, jnp.arange(N_ROW, dtype=jnp.int32))
        left = jnp.transpose(left.reshape(N, N, hidden), (2, 0, 1))
        right = jnp.transpose(right.reshape(N, N, hidden), (2, 0, 1))
        gate = gate.reshape(N, N, gate.shape[-1])

        def channel(operands):
            left_one = operands[0].astype(jnp.float32)
            right_one = operands[1].astype(jnp.float32)
            if incoming:
                return jnp.dot(left_one.T, right_one, precision=lax.Precision.HIGHEST)
            return jnp.dot(left_one, right_one.T, precision=lax.Precision.HIGHEST)
        mixed = lax.map(channel, (left, right)).astype(jnp.bfloat16)
        mixed = jnp.transpose(mixed, (1, 2, 0))
        mixnormed = layer_norm(mixed.astype(jnp.float32), mix_gain).astype(jnp.bfloat16)
        change = jnp.dot(mixnormed, final_w, preferred_element_type=jnp.float32)
        return (current.astype(jnp.float32) + jax.nn.sigmoid(gate) * change).astype(jnp.bfloat16)
    after_one = update(pair, out_norm, out_proj, out_gate, out_mix_norm, out_final, False)
    after_two = update(after_one, inc_norm, inc_proj, inc_gate, inc_mix_norm, inc_final, True)
    width = transition_down.shape[0]

    def transition(block):
        start = (block * rows).astype(jnp.int32)
        piece = lax.dynamic_slice_in_dim(after_two, start, rows, 0)
        normed = layer_norm(piece.astype(jnp.float32), transition_norm).astype(jnp.bfloat16)
        lifted = jnp.dot(normed, transition_up, preferred_element_type=jnp.float32)
        inner = (jax.nn.silu(lifted[..., :width]) * lifted[..., width:]).astype(jnp.bfloat16)
        change = jnp.dot(inner, transition_down, preferred_element_type=jnp.float32)
        return (piece.astype(jnp.float32) + change).astype(jnp.bfloat16)
    result = lax.map(transition, jnp.arange(N_ROW, dtype=jnp.int32))
    return result.reshape(N, N, result.shape[-1])
```

```python
import functools

import jax
import jax.numpy as jnp
from jax import lax
from jax.experimental import pallas as pl
from jax.experimental.pallas import tpu as pltpu
from jax.sharding import PartitionSpec as P

MESH = pl.DeviceIdType.MESH


def layer_norm(values, gain, axis):
    mean = jnp.mean(values, axis=axis, keepdims=True)
    centred = values - mean
    spread = jnp.mean(centred * centred, axis=axis, keepdims=True)
    return centred * lax.rsqrt(spread + 1e-05) * gain


def project(current, norm_gain, proj_w, gate_w, mask, form):
    normed = layer_norm(current.astype(jnp.float32), norm_gain, -1).astype(jnp.bfloat16)
    hidden = proj_w.shape[1] // 4
    left_part = jnp.einsum(
        form, normed, proj_w[:, : 2 * hidden], preferred_element_type=jnp.float32
    )
    left = (mask * jax.nn.sigmoid(left_part[:hidden]) * left_part[hidden:]).astype(jnp.bfloat16)
    right_part = jnp.einsum(
        form, normed, proj_w[:, 2 * hidden :], preferred_element_type=jnp.float32
    )
    right = (mask * jax.nn.sigmoid(right_part[:hidden]) * right_part[hidden:]).astype(jnp.bfloat16)
    gate = jnp.einsum("ijc,cd->ijd", normed, gate_w, preferred_element_type=jnp.float32)
    return (left, right, gate)


def finish(current, mixed, mix_gain, final_w, gate, form):
    mixnormed = layer_norm(mixed.astype(jnp.float32), mix_gain[:, None, None], 0).astype(
        jnp.bfloat16
    )
    change = jnp.einsum(form, mixnormed, final_w, preferred_element_type=jnp.float32)
    return (current.astype(jnp.float32) + jax.nn.sigmoid(gate) * change).astype(jnp.bfloat16)


def mix_over_col(left, right, incoming):
    left_wide, right_wide = (
        lax.all_to_all(left, "col", split_axis=0, concat_axis=2, tiled=True),
        lax.all_to_all(right, "col", split_axis=0, concat_axis=2, tiled=True),
    )
    if incoming:
        left_swapped = lax.all_to_all(left_wide, "row", split_axis=2, concat_axis=1, tiled=True)
        mixed = jnp.einsum(
            "hki,hkj->hij",
            left_swapped,
            lax.all_gather(right_wide, "row", axis=1, tiled=True),
            preferred_element_type=jnp.float32,
        )
    else:
        mixed = jnp.einsum(
            "hik,hjk->hij",
            left_wide,
            lax.all_gather(right_wide, "row", axis=1, tiled=True),
            preferred_element_type=jnp.float32,
        )
    return lax.all_to_all(
        mixed.astype(jnp.bfloat16), "col", split_axis=2, concat_axis=0, tiled=True
    )


def triangle(current, norm_gain, proj_w, gate_w, mix_gain, final_w, mask, incoming):
    left, right, gate = project(current, norm_gain, proj_w, gate_w, mask, "ijc,cf->fij")
    mixed = mix_over_col(left, right, incoming)
    return finish(current, mixed, mix_gain, final_w, gate, "hij,hc->ijc")


def local_plain(
    pair,
    residue_count,
    out_norm,
    out_proj,
    out_gate,
    out_mix_norm,
    out_final,
    inc_norm,
    inc_proj,
    inc_gate,
    inc_mix_norm,
    inc_final,
    transition_norm,
    transition_up,
    transition_down,
):
    tile_rows = pair.shape[0]
    tile_cols = pair.shape[1]
    row_place = lax.axis_index("row") * tile_rows + jnp.arange(tile_rows, dtype=jnp.int32)
    col_place = lax.axis_index("col") * tile_cols + jnp.arange(tile_cols, dtype=jnp.int32)
    valid_rows = (row_place < residue_count[0]).astype(jnp.float32)
    valid_cols = (col_place < residue_count[0]).astype(jnp.float32)
    mask = valid_rows[:, None] * valid_cols[None, :]
    after_one = triangle(pair, out_norm, out_proj, out_gate, out_mix_norm, out_final, mask, False)
    after_two = triangle(
        after_one, inc_norm, inc_proj, inc_gate, inc_mix_norm, inc_final, mask, True
    )
    normed = layer_norm(after_two.astype(jnp.float32), transition_norm, -1).astype(jnp.bfloat16)
    width = transition_down.shape[0]
    total = jnp.zeros(after_two.shape, jnp.float32)
    for offset in range(0, width, 128):
        gate_part = jnp.einsum(
            "ijc,cf->ijf",
            normed,
            transition_up[:, offset : offset + 128],
            preferred_element_type=jnp.float32,
        )
        value_part = jnp.einsum(
            "ijc,cf->ijf",
            normed,
            transition_up[:, width + offset : width + offset + 128],
            preferred_element_type=jnp.float32,
        )
        inner = (jax.nn.silu(gate_part) * value_part).astype(jnp.bfloat16)
        total = total + jnp.einsum(
            "ijf,fc->ijc",
            inner,
            transition_down[offset : offset + 128],
            preferred_element_type=jnp.float32,
        )
    return (after_two.astype(jnp.float32) + total).astype(jnp.bfloat16)


def norm_rows(values, gain):
    mean = jnp.mean(values, axis=-1, keepdims=True)
    centred = values - mean
    spread = jnp.mean(centred * centred, axis=-1, keepdims=True)
    return centred * lax.rsqrt(spread + 1e-05) * gain


def matmul(left, right):
    return jnp.dot(left, right, preferred_element_type=jnp.float32)


def masked_half(normed, proj_ref, start, hidden, mask):
    part = matmul(normed, proj_ref[:, start : start + 2 * hidden])
    return (mask * jax.nn.sigmoid(part[:, :hidden]) * part[:, hidden:]).astype(jnp.bfloat16)


def contract(size, left_ref, right_ref, out_ref, out_slot):
    for first in range(0, size, 8):

        def step(k, totals, first=first):
            base = pl.multiple_of(k * size, 8)
            block = right_ref[pl.ds(base, size), :]
            return tuple(
                total + left_ref[pl.ds(base + first + place, 1), :] * block
                for place, total in enumerate(totals)
            )

        zero = jnp.zeros((size, right_ref.shape[1]), jnp.float32)
        totals = lax.fori_loop(0, size, step, (zero,) * 8, unroll=2)
        out_ref[out_slot, first * size : (first + 8) * size, :] = jnp.concatenate(
            totals, axis=0
        ).astype(jnp.bfloat16)


def block_kernel(
    size,
    n_row,
    n_col,
    count_ref,
    pair_ref,
    out_norm,
    out_proj,
    out_gate,
    out_mix_norm,
    out_final,
    inc_norm,
    inc_proj,
    inc_gate,
    inc_mix_norm,
    inc_final,
    transition_norm,
    transition_up,
    transition_down,
    result_ref,
    turn_a,
    turn_b,
    wide_left,
    wide_right,
    right_in,
    part_out,
    part_in,
    left_in,
    sum_out,
    sum_in,
    send_a,
    recv_a,
    send_b,
    recv_b,
    send_c,
    recv_c,
    send_d,
    recv_d,
):
    row = lax.axis_index("row")
    col = lax.axis_index("col")
    tokens = size * size
    hidden = out_proj.shape[1] // 4

    def row_peer(step):
        place = (row // 2 + step // 2) % (n_row // 2)
        return place * 2 + (row % 2 + step % 2) % 2

    def col_peer(step):
        return (col + step) % n_col

    barrier = pltpu.get_barrier_semaphore()
    for step in range(1, n_row):
        pl.semaphore_signal(
            barrier, inc=1, device_id={"row": row_peer(step)}, device_id_type=MESH
        )
    for step in range(1, n_col):
        pl.semaphore_signal(
            barrier, inc=1, device_id={"col": col_peer(step)}, device_id_type=MESH
        )

    def copy(source, target, send, recv, where):
        return pltpu.make_async_remote_copy(
            src_ref=source,
            dst_ref=target,
            send_sem=send,
            recv_sem=recv,
            device_id=where,
            device_id_type=MESH,
        )

    def to_row(step):
        return copy(
            right_in.at[0], right_in.at[step], send_a.at[step], recv_a.at[step],
            {"row": row_peer(step)},
        )

    def to_owner(step):
        return copy(
            part_out.at[step], part_in.at[col], send_b.at[step], recv_b.at[col],
            {"col": row_peer(step)},
        )

    def from_col(sender):
        return copy(
            part_out.at[0], part_in.at[sender], send_b.at[0], recv_b.at[sender],
            {"col": sender},
        )

    def to_col(step):
        return copy(
            left_in.at[col], left_in.at[col], send_c.at[step], recv_c.at[col],
            {"col": col_peer(step)},
        )

    def left_from(sender):
        return copy(
            left_in.at[col], left_in.at[sender], send_c.at[0], recv_c.at[sender],
            {"col": sender},
        )

    def to_row_owner(step):
        return copy(
            sum_out.at[step], sum_in.at[row], send_d.at[step], recv_d.at[row],
            {"row": col_peer(step)},
        )

    def from_row(sender):
        return copy(
            sum_out.at[0], sum_in.at[sender], send_d.at[0], recv_d.at[sender],
            {"row": sender},
        )

    shape = (size, size, hidden)
    first = lax.broadcasted_iota(jnp.int32, shape, 0)
    second = lax.broadcasted_iota(jnp.int32, shape, 1)
    count = count_ref[0]

    def mask_of(a, b):
        real = jnp.logical_and(a < count, b < count)
        return jnp.where(real, 1.0, 0.0).astype(jnp.float32).reshape(tokens, hidden)

    mask = mask_of(first + row * size, second + col * size)
    mask_turned = mask_of(first + col * size, second + row * size)

    normed = norm_rows(pair_ref[...].astype(jnp.float32), out_norm[...])
    turn_a[...] = normed
    for k in range(size):
        turn_b[k * size : (k + 1) * size, :] = turn_a[pl.ds(k, size, stride=size), :]
    turned = turn_b[...].astype(jnp.bfloat16)
    right_in[0] = masked_half(turned, out_proj, 2 * hidden, hidden, mask_turned)
    pl.semaphore_wait(barrier, n_row + n_col - 2)
    for step in range(1, n_row):
        to_row(step).start()
    wide_left[...] = masked_half(turned, out_proj, 0, hidden, mask_turned).astype(jnp.float32)
    for step in range(n_row):
        if step > 0:
            to_row(step).wait_recv()
        wide_right[...] = right_in[step].astype(jnp.float32)
        contract(size, wide_left, wide_right, part_out, step)

        @pl.when(row_peer(step) != col)
        def _():
            to_owner(step).start()

        @pl.when(row_peer(step) == col)
        def _():
            part_in[col] = part_out[step]

    gate = jax.nn.sigmoid(matmul(normed.astype(jnp.bfloat16), out_gate[...]))
    for sender in range(n_col):

        @pl.when(sender != col)
        def _():
            from_col(sender).wait_recv()

    mixed = part_in[0].astype(jnp.float32)
    for sender in range(1, n_col):
        mixed = mixed + part_in[sender].astype(jnp.float32)
    mixed = norm_rows(mixed.astype(jnp.bfloat16).astype(jnp.float32), out_mix_norm[...])
    change = matmul(mixed.astype(jnp.bfloat16), out_final[...])
    after = (pair_ref[...].astype(jnp.float32) + gate * change).astype(jnp.bfloat16)
    after = after.astype(jnp.float32)

    normed = norm_rows(after, inc_norm[...]).astype(jnp.bfloat16)
    left_in[col] = masked_half(normed, inc_proj, 0, hidden, mask)
    for step in range(1, n_col):
        to_col(step).start()
    wide_right[...] = masked_half(normed, inc_proj, 2 * hidden, hidden, mask).astype(jnp.float32)
    gate = jax.nn.sigmoid(matmul(normed, inc_gate[...]))
    turn_a[...] = after
    turn_b[...] = gate
    for step in (0, 1, 3, 2):
        owner = col_peer(step)
        if step > 0:
            left_from(owner).wait_recv()
        wide_left[...] = left_in[owner].astype(jnp.float32)
        contract(size, wide_left, wide_right, sum_out, step)

        @pl.when(owner != row)
        def _():
            to_row_owner(step).start()

        @pl.when(owner == row)
        def _():
            sum_in[row] = sum_out[step]

    for sender in range(n_row):

        @pl.when(sender != row)
        def _():
            from_row(sender).wait_recv()

    mixed = sum_in[0].astype(jnp.float32)
    for sender in range(1, n_row):
        mixed = mixed + sum_in[sender].astype(jnp.float32)
    mixed = norm_rows(mixed.astype(jnp.bfloat16).astype(jnp.float32), inc_mix_norm[...])
    change = matmul(mixed.astype(jnp.bfloat16), inc_final[...])
    after = (turn_a[...] + turn_b[...] * change).astype(jnp.bfloat16).astype(jnp.float32)

    normed = norm_rows(after, transition_norm[...]).astype(jnp.bfloat16)
    width = transition_down.shape[0]
    total = jnp.zeros((tokens, hidden), jnp.float32)
    for offset in range(0, width, 256):
        lifted = matmul(normed, transition_up[:, offset : offset + 256])
        value = matmul(normed, transition_up[:, width + offset : width + offset + 256])
        inner = (lifted * jax.nn.sigmoid(lifted) * value).astype(jnp.bfloat16)
        total = total + matmul(inner, transition_down[offset : offset + 256, :])
    result_ref[...] = (after + total.astype(jnp.bfloat16).astype(jnp.float32)).astype(jnp.bfloat16)

    for step in range(1, n_row):
        to_row(step).wait_send()
    for step in range(n_row):

        @pl.when(row_peer(step) != col)
        def _():
            to_owner(step).wait_send()

    for step in range(1, n_col):
        to_col(step).wait_send()
    for step in range(n_col):

        @pl.when(col_peer(step) != row)
        def _():
            to_row_owner(step).wait_send()


def local_kernel(n_row, n_col, pair, residue_count, *rest):
    size, _, channels = pair.shape
    tokens = size * size
    rest = [leaf[None, :] if leaf.ndim == 1 else leaf for leaf in rest]
    vmem = pl.BlockSpec(memory_space=pltpu.VMEM)
    narrow = pltpu.VMEM((4, tokens, channels), jnp.bfloat16)
    wide = pltpu.VMEM((tokens, channels), jnp.float32)
    result = pl.pallas_call(
        functools.partial(block_kernel, size, n_row, n_col),
        out_shape=jax.ShapeDtypeStruct((tokens, channels), jnp.bfloat16),
        in_specs=[pl.BlockSpec(memory_space=pltpu.SMEM)] + [vmem] * (1 + len(rest)),
        out_specs=vmem,
        scratch_shapes=[wide] * 4 + [narrow] * 6 + [pltpu.SemaphoreType.DMA((4,))] * 8,
        compiler_params=pltpu.CompilerParams(
            collective_id=0, has_side_effects=True, vmem_limit_bytes=48 * 1024 * 1024
        ),
    )(residue_count, pair.reshape(tokens, channels), *rest)
    return result.reshape(size, size, channels)


def local(pair, residue_count, *rest, n_row, n_col):
    hidden = rest[1].shape[1] // 4
    fits = n_row == 4 and n_col == 4 and pair.shape[0] == pair.shape[1]
    fits = fits and pair.shape[0] % 8 == 0 and pair.shape[0] <= 32
    if fits and hidden == pair.shape[2] and hidden % 128 == 0:
        return local_kernel(n_row, n_col, pair, residue_count, *rest)
    return local_plain(pair, residue_count, *rest)


def solution(mesh):
    placed = (
        P(("parts", "row"), "col", None),
        P("parts"),
        P(),
        P(),
        P(),
        P(),
        P(),
        P(),
        P(),
        P(),
        P(),
        P(),
        P(),
        P(),
        P(),
    )
    return jax.shard_map(
        functools.partial(
            local, n_row=mesh.shape["row"], n_col=mesh.shape["col"]
        ),
        mesh=mesh,
        in_specs=placed,
        out_specs=P(("parts", "row"), "col", None),
        check_vma=False,
    )
```

```python
import functools

import jax
import jax.numpy as jnp
from jax import lax
from jax.experimental import pallas as pl
from jax.experimental.pallas import tpu as pltpu
from jax.sharding import PartitionSpec as P

MESH = pl.DeviceIdType.MESH


def layer_norm(values, gain, axis):
    mean = jnp.mean(values, axis=axis, keepdims=True)
    centred = values - mean
    spread = jnp.mean(centred * centred, axis=axis, keepdims=True)
    return centred * lax.rsqrt(spread + 1e-05) * gain


def project(current, norm_gain, proj_w, gate_w, mask, form):
    normed = layer_norm(current.astype(jnp.float32), norm_gain, -1).astype(jnp.bfloat16)
    hidden = proj_w.shape[1] // 4
    left_part = jnp.einsum(
        form, normed, proj_w[:, : 2 * hidden], preferred_element_type=jnp.float32
    )
    left = (mask * jax.nn.sigmoid(left_part[:hidden]) * left_part[hidden:]).astype(jnp.bfloat16)
    right_part = jnp.einsum(
        form, normed, proj_w[:, 2 * hidden :], preferred_element_type=jnp.float32
    )
    right = (mask * jax.nn.sigmoid(right_part[:hidden]) * right_part[hidden:]).astype(jnp.bfloat16)
    gate = jnp.einsum("ijc,cd->ijd", normed, gate_w, preferred_element_type=jnp.float32)
    return (left, right, gate)


def finish(current, mixed, mix_gain, final_w, gate, form):
    mixnormed = layer_norm(mixed.astype(jnp.float32), mix_gain[:, None, None], 0).astype(
        jnp.bfloat16
    )
    change = jnp.einsum(form, mixnormed, final_w, preferred_element_type=jnp.float32)
    return (current.astype(jnp.float32) + jax.nn.sigmoid(gate) * change).astype(jnp.bfloat16)


def mix_over_col(left, right, incoming):
    left_wide, right_wide = (
        lax.all_to_all(left, "col", split_axis=0, concat_axis=2, tiled=True),
        lax.all_to_all(right, "col", split_axis=0, concat_axis=2, tiled=True),
    )
    if incoming:
        left_swapped = lax.all_to_all(left_wide, "row", split_axis=2, concat_axis=1, tiled=True)
        mixed = jnp.einsum(
            "hki,hkj->hij",
            left_swapped,
            lax.all_gather(right_wide, "row", axis=1, tiled=True),
            preferred_element_type=jnp.float32,
        )
    else:
        mixed = jnp.einsum(
            "hik,hjk->hij",
            left_wide,
            lax.all_gather(right_wide, "row", axis=1, tiled=True),
            preferred_element_type=jnp.float32,
        )
    return lax.all_to_all(
        mixed.astype(jnp.bfloat16), "col", split_axis=2, concat_axis=0, tiled=True
    )


def triangle(current, norm_gain, proj_w, gate_w, mix_gain, final_w, mask, incoming):
    left, right, gate = project(current, norm_gain, proj_w, gate_w, mask, "ijc,cf->fij")
    mixed = mix_over_col(left, right, incoming)
    return finish(current, mixed, mix_gain, final_w, gate, "hij,hc->ijc")


def local_plain(
    pair,
    residue_count,
    out_norm,
    out_proj,
    out_gate,
    out_mix_norm,
    out_final,
    inc_norm,
    inc_proj,
    inc_gate,
    inc_mix_norm,
    inc_final,
    transition_norm,
    transition_up,
    transition_down,
):
    tile_rows = pair.shape[0]
    tile_cols = pair.shape[1]
    row_place = lax.axis_index("row") * tile_rows + jnp.arange(tile_rows, dtype=jnp.int32)
    col_place = lax.axis_index("col") * tile_cols + jnp.arange(tile_cols, dtype=jnp.int32)
    valid_rows = (row_place < residue_count[0]).astype(jnp.float32)
    valid_cols = (col_place < residue_count[0]).astype(jnp.float32)
    mask = valid_rows[:, None] * valid_cols[None, :]
    after_one = triangle(pair, out_norm, out_proj, out_gate, out_mix_norm, out_final, mask, False)
    after_two = triangle(
        after_one, inc_norm, inc_proj, inc_gate, inc_mix_norm, inc_final, mask, True
    )
    normed = layer_norm(after_two.astype(jnp.float32), transition_norm, -1).astype(jnp.bfloat16)
    width = transition_down.shape[0]
    total = jnp.zeros(after_two.shape, jnp.float32)
    for offset in range(0, width, 128):
        gate_part = jnp.einsum(
            "ijc,cf->ijf",
            normed,
            transition_up[:, offset : offset + 128],
            preferred_element_type=jnp.float32,
        )
        value_part = jnp.einsum(
            "ijc,cf->ijf",
            normed,
            transition_up[:, width + offset : width + offset + 128],
            preferred_element_type=jnp.float32,
        )
        inner = (jax.nn.silu(gate_part) * value_part).astype(jnp.bfloat16)
        total = total + jnp.einsum(
            "ijf,fc->ijc",
            inner,
            transition_down[offset : offset + 128],
            preferred_element_type=jnp.float32,
        )
    return (after_two.astype(jnp.float32) + total).astype(jnp.bfloat16)


def norm_rows(values, gain):
    mean = jnp.mean(values, axis=-1, keepdims=True)
    centred = values - mean
    spread = jnp.mean(centred * centred, axis=-1, keepdims=True)
    return centred * lax.rsqrt(spread + 1e-05) * gain


def matmul(left, right):
    return jnp.dot(left, right, preferred_element_type=jnp.float32)


def masked_half(normed, proj_ref, start, hidden, mask):
    part = matmul(normed, proj_ref[:, start : start + 2 * hidden])
    return (mask * jax.nn.sigmoid(part[:, :hidden]) * part[:, hidden:]).astype(jnp.bfloat16)


def contract(size, left_ref, right_ref, out_ref, out_slot):
    for first in range(0, size, 8):

        def step(k, totals, first=first):
            base = pl.multiple_of(k * size, 8)
            block = right_ref[pl.ds(base, size), :]
            return tuple(
                total + left_ref[pl.ds(base + first + place, 1), :] * block
                for place, total in enumerate(totals)
            )

        zero = jnp.zeros((size, right_ref.shape[1]), jnp.float32)
        totals = lax.fori_loop(0, size, step, (zero,) * 8, unroll=2)
        out_ref[out_slot, first * size : (first + 8) * size, :] = jnp.concatenate(
            totals, axis=0
        ).astype(jnp.bfloat16)


def block_kernel(
    size,
    n_row,
    n_col,
    count_ref,
    *refs,
):
    sources, result_ref, held, refs = refs[:14], refs[14], refs[15:29], refs[29:]
    (
        pair_ref,
        out_norm,
        out_proj,
        out_gate,
        out_mix_norm,
        out_final,
        inc_norm,
        inc_proj,
        inc_gate,
        inc_mix_norm,
        inc_final,
        transition_norm,
        transition_up,
        transition_down,
    ) = held
    (
        turn_a,
        turn_b,
        wide_left,
        wide_right,
        right_in,
        part_out,
        part_in,
        left_in,
        sum_out,
        sum_in,
        send_a,
        recv_a,
        send_b,
        recv_b,
        send_c,
        recv_c,
        send_d,
        recv_d,
        load,
    ) = refs
    row = lax.axis_index("row")
    col = lax.axis_index("col")
    tokens = size * size
    hidden = out_proj.shape[1] // 4

    loads = [
        pltpu.make_async_copy(source, target, load.at[place])
        for place, (source, target) in enumerate(zip(sources, held))
    ]
    for one in loads:
        one.start()

    def row_peer(step):
        place = (row // 2 + step // 2) % (n_row // 2)
        return place * 2 + (row % 2 + step % 2) % 2

    def col_peer(step):
        return (col + step) % n_col

    barrier = pltpu.get_barrier_semaphore()
    for step in range(1, n_row):
        pl.semaphore_signal(
            barrier, inc=1, device_id={"row": row_peer(step)}, device_id_type=MESH
        )
    for step in range(1, n_col):
        pl.semaphore_signal(
            barrier, inc=1, device_id={"col": col_peer(step)}, device_id_type=MESH
        )

    def copy(source, target, send, recv, where):
        return pltpu.make_async_remote_copy(
            src_ref=source,
            dst_ref=target,
            send_sem=send,
            recv_sem=recv,
            device_id=where,
            device_id_type=MESH,
        )

    def to_row(step):
        hop = 1 if step == 3 else step
        return copy(
            right_in.at[step - hop], right_in.at[step], send_a.at[step], recv_a.at[step],
            {"row": row_peer(hop)},
        )

    def to_owner(step):
        return copy(
            part_out.at[step], part_in.at[col], send_b.at[step], recv_b.at[col],
            {"col": row_peer(step)},
        )

    def from_col(sender):
        return copy(
            part_out.at[0], part_in.at[sender], send_b.at[0], recv_b.at[sender],
            {"col": sender},
        )

    def to_col(step):
        return copy(
            left_in.at[col], left_in.at[col], send_c.at[step], recv_c.at[col],
            {"col": col_peer(step)},
        )

    def left_from(sender):
        return copy(
            left_in.at[col], left_in.at[sender], send_c.at[0], recv_c.at[sender],
            {"col": sender},
        )

    def to_row_owner(step):
        return copy(
            sum_out.at[step], sum_in.at[row], send_d.at[step], recv_d.at[row],
            {"row": col_peer(step)},
        )

    def from_row(sender):
        return copy(
            sum_out.at[0], sum_in.at[sender], send_d.at[0], recv_d.at[sender],
            {"row": sender},
        )

    shape = (size, size, hidden)
    first = lax.broadcasted_iota(jnp.int32, shape, 0)
    second = lax.broadcasted_iota(jnp.int32, shape, 1)
    count = count_ref[0]

    def mask_of(a, b):
        real = jnp.logical_and(a < count, b < count)
        return jnp.where(real, 1.0, 0.0).astype(jnp.float32).reshape(tokens, hidden)

    mask = mask_of(first + row * size, second + col * size)
    mask_turned = mask_of(first + col * size, second + row * size)

    for one in loads[:3]:
        one.wait()
    normed = norm_rows(pair_ref[...].astype(jnp.float32), out_norm[...])
    turn_a[...] = normed
    for k in range(size):
        turn_b[k * size : (k + 1) * size, :] = turn_a[pl.ds(k, size, stride=size), :]
    turned = turn_b[...].astype(jnp.bfloat16)
    right_in[0] = masked_half(turned, out_proj, 2 * hidden, hidden, mask_turned)
    pl.semaphore_wait(barrier, n_row + n_col - 2)
    for step in (2, 1):
        to_row(step).start()
    wide_left[...] = masked_half(turned, out_proj, 0, hidden, mask_turned).astype(jnp.float32)
    for step in range(n_row):
        if step > 0:
            to_row(step).wait_recv()
        if step == 2:
            to_row(3).start()
        wide_right[...] = right_in[step].astype(jnp.float32)
        contract(size, wide_left, wide_right, part_out, step)

        @pl.when(row_peer(step) != col)
        def _():
            to_owner(step).start()

        @pl.when(row_peer(step) == col)
        def _():
            part_in[col] = part_out[step]

    for one in loads[3:6]:
        one.wait()
    gate = jax.nn.sigmoid(matmul(normed.astype(jnp.bfloat16), out_gate[...]))
    for sender in range(n_col):

        @pl.when(sender != col)
        def _():
            from_col(sender).wait_recv()

    mixed = part_in[0].astype(jnp.float32)
    for sender in range(1, n_col):
        mixed = mixed + part_in[sender].astype(jnp.float32)
    mixed = norm_rows(mixed.astype(jnp.bfloat16).astype(jnp.float32), out_mix_norm[...])
    change = matmul(mixed.astype(jnp.bfloat16), out_final[...])
    after = (pair_ref[...].astype(jnp.float32) + gate * change).astype(jnp.bfloat16)
    after = after.astype(jnp.float32)

    for one in loads[6:]:
        one.wait()
    normed = norm_rows(after, inc_norm[...]).astype(jnp.bfloat16)
    left_in[col] = masked_half(normed, inc_proj, 0, hidden, mask)
    for step in range(1, n_col):
        to_col(step).start()
    wide_right[...] = masked_half(normed, inc_proj, 2 * hidden, hidden, mask).astype(jnp.float32)
    gate = jax.nn.sigmoid(matmul(normed, inc_gate[...]))
    turn_a[...] = after
    turn_b[...] = gate
    for step in (0, 1, 3, 2):
        owner = col_peer(step)
        if step > 0:
            left_from(owner).wait_recv()
        wide_left[...] = left_in[owner].astype(jnp.float32)
        contract(size, wide_left, wide_right, sum_out, step)

        @pl.when(owner != row)
        def _():
            to_row_owner(step).start()

        @pl.when(owner == row)
        def _():
            sum_in[row] = sum_out[step]

    for sender in range(n_row):

        @pl.when(sender != row)
        def _():
            from_row(sender).wait_recv()

    mixed = sum_in[0].astype(jnp.float32)
    for sender in range(1, n_row):
        mixed = mixed + sum_in[sender].astype(jnp.float32)
    mixed = norm_rows(mixed.astype(jnp.bfloat16).astype(jnp.float32), inc_mix_norm[...])
    change = matmul(mixed.astype(jnp.bfloat16), inc_final[...])
    after = (turn_a[...] + turn_b[...] * change).astype(jnp.bfloat16).astype(jnp.float32)

    normed = norm_rows(after, transition_norm[...]).astype(jnp.bfloat16)
    width = transition_down.shape[0]
    total = jnp.zeros((tokens, hidden), jnp.float32)
    for offset in range(0, width, 256):
        lifted = matmul(normed, transition_up[:, offset : offset + 256])
        value = matmul(normed, transition_up[:, width + offset : width + offset + 256])
        inner = (lifted * jax.nn.sigmoid(lifted) * value).astype(jnp.bfloat16)
        total = total + matmul(inner, transition_down[offset : offset + 256, :])
    result_ref[...] = (after + total.astype(jnp.bfloat16).astype(jnp.float32)).astype(jnp.bfloat16)

    for step in range(1, n_row):
        to_row(step).wait_send()
    for step in range(n_row):

        @pl.when(row_peer(step) != col)
        def _():
            to_owner(step).wait_send()

    for step in range(1, n_col):
        to_col(step).wait_send()
    for step in range(n_col):

        @pl.when(col_peer(step) != row)
        def _():
            to_row_owner(step).wait_send()


def local_kernel(n_row, n_col, pair, residue_count, *rest):
    size, _, channels = pair.shape
    tokens = size * size
    rest = [leaf[None, :] if leaf.ndim == 1 else leaf for leaf in rest]
    operands = [pair.reshape(tokens, channels)] + rest
    vmem = pl.BlockSpec(memory_space=pltpu.VMEM)
    hbm = pl.BlockSpec(memory_space=pltpu.HBM)
    narrow = pltpu.VMEM((4, tokens, channels), jnp.bfloat16)
    wide = pltpu.VMEM((tokens, channels), jnp.float32)
    result = pl.pallas_call(
        functools.partial(block_kernel, size, n_row, n_col),
        out_shape=jax.ShapeDtypeStruct((tokens, channels), jnp.bfloat16),
        in_specs=[pl.BlockSpec(memory_space=pltpu.SMEM)] + [hbm] * len(operands),
        out_specs=vmem,
        scratch_shapes=[pltpu.VMEM(leaf.shape, leaf.dtype) for leaf in operands]
        + [wide] * 4
        + [narrow] * 6
        + [pltpu.SemaphoreType.DMA((4,))] * 8
        + [pltpu.SemaphoreType.DMA((len(operands),))],
        compiler_params=pltpu.CompilerParams(
            collective_id=0, has_side_effects=True, vmem_limit_bytes=62 * 1024 * 1024
        ),
    )(residue_count, *operands)
    return result.reshape(size, size, channels)


def local(pair, residue_count, *rest, n_row, n_col):
    hidden = rest[1].shape[1] // 4
    fits = n_row == 4 and n_col == 4 and pair.shape[0] == pair.shape[1]
    fits = fits and pair.shape[0] % 8 == 0 and pair.shape[0] <= 32
    if fits and hidden == pair.shape[2] and hidden % 128 == 0:
        return local_kernel(n_row, n_col, pair, residue_count, *rest)
    return local_plain(pair, residue_count, *rest)


def solution(mesh):
    placed = (
        P(("parts", "row"), "col", None),
        P("parts"),
        P(),
        P(),
        P(),
        P(),
        P(),
        P(),
        P(),
        P(),
        P(),
        P(),
        P(),
        P(),
        P(),
    )
    return jax.shard_map(
        functools.partial(
            local, n_row=mesh.shape["row"], n_col=mesh.shape["col"]
        ),
        mesh=mesh,
        in_specs=placed,
        out_specs=P(("parts", "row"), "col", None),
        check_vma=False,
    )
```

```python
import functools

import jax
import jax.numpy as jnp
from jax import lax
from jax.experimental import pallas as pl
from jax.experimental.pallas import tpu as pltpu
from jax.sharding import PartitionSpec as P

MESH = pl.DeviceIdType.MESH


def layer_norm(values, gain, axis):
    mean = jnp.mean(values, axis=axis, keepdims=True)
    centred = values - mean
    spread = jnp.mean(centred * centred, axis=axis, keepdims=True)
    return centred * lax.rsqrt(spread + 1e-05) * gain


def project(current, norm_gain, proj_w, gate_w, mask, form):
    normed = layer_norm(current.astype(jnp.float32), norm_gain, -1).astype(jnp.bfloat16)
    hidden = proj_w.shape[1] // 4
    left_part = jnp.einsum(
        form, normed, proj_w[:, : 2 * hidden], preferred_element_type=jnp.float32
    )
    left = (mask * jax.nn.sigmoid(left_part[:hidden]) * left_part[hidden:]).astype(jnp.bfloat16)
    right_part = jnp.einsum(
        form, normed, proj_w[:, 2 * hidden :], preferred_element_type=jnp.float32
    )
    right = (mask * jax.nn.sigmoid(right_part[:hidden]) * right_part[hidden:]).astype(jnp.bfloat16)
    gate = jnp.einsum("ijc,cd->ijd", normed, gate_w, preferred_element_type=jnp.float32)
    return (left, right, gate)


def finish(current, mixed, mix_gain, final_w, gate, form):
    mixnormed = layer_norm(mixed.astype(jnp.float32), mix_gain[:, None, None], 0).astype(
        jnp.bfloat16
    )
    change = jnp.einsum(form, mixnormed, final_w, preferred_element_type=jnp.float32)
    return (current.astype(jnp.float32) + jax.nn.sigmoid(gate) * change).astype(jnp.bfloat16)


def mix_over_col(left, right, incoming):
    left_wide, right_wide = (
        lax.all_to_all(left, "col", split_axis=0, concat_axis=2, tiled=True),
        lax.all_to_all(right, "col", split_axis=0, concat_axis=2, tiled=True),
    )
    if incoming:
        left_swapped = lax.all_to_all(left_wide, "row", split_axis=2, concat_axis=1, tiled=True)
        mixed = jnp.einsum(
            "hki,hkj->hij",
            left_swapped,
            lax.all_gather(right_wide, "row", axis=1, tiled=True),
            preferred_element_type=jnp.float32,
        )
    else:
        mixed = jnp.einsum(
            "hik,hjk->hij",
            left_wide,
            lax.all_gather(right_wide, "row", axis=1, tiled=True),
            preferred_element_type=jnp.float32,
        )
    return lax.all_to_all(
        mixed.astype(jnp.bfloat16), "col", split_axis=2, concat_axis=0, tiled=True
    )


def triangle(current, norm_gain, proj_w, gate_w, mix_gain, final_w, mask, incoming):
    left, right, gate = project(current, norm_gain, proj_w, gate_w, mask, "ijc,cf->fij")
    mixed = mix_over_col(left, right, incoming)
    return finish(current, mixed, mix_gain, final_w, gate, "hij,hc->ijc")


def local_plain(
    pair,
    residue_count,
    out_norm,
    out_proj,
    out_gate,
    out_mix_norm,
    out_final,
    inc_norm,
    inc_proj,
    inc_gate,
    inc_mix_norm,
    inc_final,
    transition_norm,
    transition_up,
    transition_down,
):
    tile_rows = pair.shape[0]
    tile_cols = pair.shape[1]
    row_place = lax.axis_index("row") * tile_rows + jnp.arange(tile_rows, dtype=jnp.int32)
    col_place = lax.axis_index("col") * tile_cols + jnp.arange(tile_cols, dtype=jnp.int32)
    valid_rows = (row_place < residue_count[0]).astype(jnp.float32)
    valid_cols = (col_place < residue_count[0]).astype(jnp.float32)
    mask = valid_rows[:, None] * valid_cols[None, :]
    after_one = triangle(pair, out_norm, out_proj, out_gate, out_mix_norm, out_final, mask, False)
    after_two = triangle(
        after_one, inc_norm, inc_proj, inc_gate, inc_mix_norm, inc_final, mask, True
    )
    normed = layer_norm(after_two.astype(jnp.float32), transition_norm, -1).astype(jnp.bfloat16)
    width = transition_down.shape[0]
    total = jnp.zeros(after_two.shape, jnp.float32)
    for offset in range(0, width, 128):
        gate_part = jnp.einsum(
            "ijc,cf->ijf",
            normed,
            transition_up[:, offset : offset + 128],
            preferred_element_type=jnp.float32,
        )
        value_part = jnp.einsum(
            "ijc,cf->ijf",
            normed,
            transition_up[:, width + offset : width + offset + 128],
            preferred_element_type=jnp.float32,
        )
        inner = (jax.nn.silu(gate_part) * value_part).astype(jnp.bfloat16)
        total = total + jnp.einsum(
            "ijf,fc->ijc",
            inner,
            transition_down[offset : offset + 128],
            preferred_element_type=jnp.float32,
        )
    return (after_two.astype(jnp.float32) + total).astype(jnp.bfloat16)


def norm_rows(values, gain):
    mean = jnp.mean(values, axis=-1, keepdims=True)
    centred = values - mean
    spread = jnp.mean(centred * centred, axis=-1, keepdims=True)
    return centred * lax.rsqrt(spread + 1e-05) * gain


def matmul(left, right):
    return jnp.dot(left, right, preferred_element_type=jnp.float32)


def masked_half(normed, proj_ref, start, hidden, mask):
    part = matmul(normed, proj_ref[:, start : start + 2 * hidden])
    return (mask * jax.nn.sigmoid(part[:, :hidden]) * part[:, hidden:]).astype(jnp.bfloat16)


def contract(size, left_ref, right_ref, out_ref, out_slot, piece):
    def step(k, totals):
        block = right_ref[pl.ds(pl.multiple_of(k * size, 8), size), :]
        base = pl.multiple_of((piece * size + k) * 8, 8)
        return tuple(
            total + left_ref[pl.ds(base + place, 1), :] * block
            for place, total in enumerate(totals)
        )

    zero = jnp.zeros((size, right_ref.shape[1]), jnp.float32)
    totals = lax.fori_loop(0, size, step, (zero,) * 8, unroll=2)
    out_ref[out_slot, piece * 8 * size : (piece + 1) * 8 * size, :] = jnp.concatenate(
        totals, axis=0
    ).astype(jnp.bfloat16)


def by_pieces(size, values, out_ref):
    for k in range(size):
        for piece in range(size // 8):
            source = k * size + piece * 8
            target = (piece * size + k) * 8
            out_ref[target : target + 8, :] = values[source : source + 8, :]


def block_kernel(
    size,
    n_row,
    n_col,
    count_ref,
    *refs,
):
    sources, result_ref, held, refs = refs[:14], refs[14], refs[15:29], refs[29:]
    (
        pair_ref,
        out_norm,
        out_proj,
        out_gate,
        out_mix_norm,
        out_final,
        inc_norm,
        inc_proj,
        inc_gate,
        inc_mix_norm,
        inc_final,
        transition_norm,
        transition_up,
        transition_down,
    ) = held
    (
        turn_a,
        turn_b,
        wide_left,
        wide_right,
        right_in,
        part_out,
        part_in,
        left_in,
        sum_out,
        sum_in,
        send_a,
        recv_a,
        send_b,
        recv_b,
        send_c,
        recv_c,
        send_d,
        recv_d,
        load,
    ) = refs
    row = lax.axis_index("row")
    col = lax.axis_index("col")
    tokens = size * size
    pieces = range(size // 8)
    hidden = out_proj.shape[1] // 4

    loads = [
        pltpu.make_async_copy(source, target, load.at[place])
        for place, (source, target) in enumerate(zip(sources, held))
    ]
    for one in loads:
        one.start()

    def row_peer(step):
        place = (row // 2 + step // 2) % (n_row // 2)
        return place * 2 + (row % 2 + step % 2) % 2

    def col_peer(step):
        return (col + step) % n_col

    barrier = pltpu.get_barrier_semaphore()
    for step in range(1, n_row):
        pl.semaphore_signal(
            barrier, inc=1, device_id={"row": row_peer(step)}, device_id_type=MESH
        )
    for step in range(1, n_col):
        pl.semaphore_signal(
            barrier, inc=1, device_id={"col": col_peer(step)}, device_id_type=MESH
        )

    def copy(source, target, send, recv, where):
        return pltpu.make_async_remote_copy(
            src_ref=source,
            dst_ref=target,
            send_sem=send,
            recv_sem=recv,
            device_id=where,
            device_id_type=MESH,
        )

    def to_row(step):
        hop = 1 if step == 3 else step
        return copy(
            right_in.at[step - hop], right_in.at[step], send_a.at[step], recv_a.at[step],
            {"row": row_peer(hop)},
        )

    def to_owner(step, piece):
        part = pl.ds(piece * 8 * size, 8 * size)
        return copy(
            part_out.at[step, part], part_in.at[col, part], send_b.at[step, piece], recv_b.at[col, piece],
            {"col": row_peer(step)},
        )

    def from_col(sender, piece):
        part = pl.ds(piece * 8 * size, 8 * size)
        return copy(
            part_out.at[0, part], part_in.at[sender, part], send_b.at[0, piece], recv_b.at[sender, piece],
            {"col": sender},
        )

    def to_col(step, piece):
        part = pl.ds(piece * 8 * size, 8 * size)
        return copy(
            left_in.at[col, part], left_in.at[col, part], send_c.at[step, piece], recv_c.at[col, piece],
            {"col": col_peer(step)},
        )

    def left_from(sender, piece):
        part = pl.ds(piece * 8 * size, 8 * size)
        return copy(
            left_in.at[col, part], left_in.at[sender, part], send_c.at[0, piece], recv_c.at[sender, piece],
            {"col": sender},
        )

    def to_row_owner(step, piece):
        part = pl.ds(piece * 8 * size, 8 * size)
        return copy(
            sum_out.at[step, part], sum_in.at[row, part], send_d.at[step, piece], recv_d.at[row, piece],
            {"row": col_peer(step)},
        )

    def from_row(sender, piece):
        part = pl.ds(piece * 8 * size, 8 * size)
        return copy(
            sum_out.at[0, part], sum_in.at[sender, part], send_d.at[0, piece], recv_d.at[sender, piece],
            {"row": sender},
        )

    shape = (size, size, hidden)
    first = lax.broadcasted_iota(jnp.int32, shape, 0)
    second = lax.broadcasted_iota(jnp.int32, shape, 1)
    count = count_ref[0]

    def mask_of(a, b):
        real = jnp.logical_and(a < count, b < count)
        return jnp.where(real, 1.0, 0.0).astype(jnp.float32).reshape(tokens, hidden)

    mask = mask_of(first + row * size, second + col * size)
    mask_turned = mask_of(first + col * size, second + row * size)

    for one in loads[:3]:
        one.wait()
    normed = norm_rows(pair_ref[...].astype(jnp.float32), out_norm[...])
    turn_a[...] = normed
    for k in range(size):
        turn_b[k * size : (k + 1) * size, :] = turn_a[pl.ds(k, size, stride=size), :]
    turned = turn_b[...].astype(jnp.bfloat16)
    right_in[0] = masked_half(turned, out_proj, 2 * hidden, hidden, mask_turned)
    pl.semaphore_wait(barrier, n_row + n_col - 2)
    for step in (2, 1):
        to_row(step).start()
    left = masked_half(turned, out_proj, 0, hidden, mask_turned)
    by_pieces(size, left.astype(jnp.float32), wide_left)
    for step in range(n_row):
        if step > 0:
            to_row(step).wait_recv()
        if step == 2:
            to_row(3).start()
        wide_right[...] = right_in[step].astype(jnp.float32)
        for piece in pieces:
            contract(size, wide_left, wide_right, part_out, step, piece)

            @pl.when(row_peer(step) != col)
            def _():
                to_owner(step, piece).start()

        @pl.when(row_peer(step) == col)
        def _():
            part_in[col] = part_out[step]

    for one in loads[3:6]:
        one.wait()
    gate = jax.nn.sigmoid(matmul(normed.astype(jnp.bfloat16), out_gate[...]))
    for sender in range(n_col):

        @pl.when(sender != col)
        def _():
            for piece in pieces:
                from_col(sender, piece).wait_recv()

    mixed = part_in[0].astype(jnp.float32)
    for sender in range(1, n_col):
        mixed = mixed + part_in[sender].astype(jnp.float32)
    mixed = norm_rows(mixed.astype(jnp.bfloat16).astype(jnp.float32), out_mix_norm[...])
    change = matmul(mixed.astype(jnp.bfloat16), out_final[...])
    after = (pair_ref[...].astype(jnp.float32) + gate * change).astype(jnp.bfloat16)
    after = after.astype(jnp.float32)

    for one in loads[6:]:
        one.wait()
    normed = norm_rows(after, inc_norm[...]).astype(jnp.bfloat16)
    left = masked_half(normed, inc_proj, 0, hidden, mask)
    by_pieces(size, left.astype(jnp.float32), wide_left)
    left_in[col] = wide_left[...].astype(jnp.bfloat16)
    for piece in pieces:
        for step in (2, 1, 3):
            to_col(step, piece).start()
    wide_right[...] = masked_half(normed, inc_proj, 2 * hidden, hidden, mask).astype(jnp.float32)
    gate = jax.nn.sigmoid(matmul(normed, inc_gate[...]))
    turn_a[...] = after
    turn_b[...] = gate
    order = [(0, piece) for piece in pieces]
    order += [(step, piece) for piece in pieces for step in (1, 3, 2)]
    for step, piece in order:
        owner = col_peer(step)
        if step > 0:
            left_from(owner, piece).wait_recv()
            part = pl.ds(piece * 8 * size, 8 * size)
            wide_left[part, :] = left_in[owner, part, :].astype(jnp.float32)
        contract(size, wide_left, wide_right, sum_out, step, piece)

        @pl.when(owner != row)
        def _():
            to_row_owner(step, piece).start()

        @pl.when(owner == row)
        def _():
            part = pl.ds(piece * 8 * size, 8 * size)
            sum_in[row, part, :] = sum_out[step, part, :]

    for sender in range(n_row):

        @pl.when(sender != row)
        def _():
            for piece in pieces:
                from_row(sender, piece).wait_recv()

    mixed = sum_in[0].astype(jnp.float32)
    for sender in range(1, n_row):
        mixed = mixed + sum_in[sender].astype(jnp.float32)
    mixed = norm_rows(mixed.astype(jnp.bfloat16).astype(jnp.float32), inc_mix_norm[...])
    change = matmul(mixed.astype(jnp.bfloat16), inc_final[...])
    after = (turn_a[...] + turn_b[...] * change).astype(jnp.bfloat16).astype(jnp.float32)

    normed = norm_rows(after, transition_norm[...]).astype(jnp.bfloat16)
    width = transition_down.shape[0]
    total = jnp.zeros((tokens, hidden), jnp.float32)
    for offset in range(0, width, 256):
        lifted = matmul(normed, transition_up[:, offset : offset + 256])
        value = matmul(normed, transition_up[:, width + offset : width + offset + 256])
        inner = (lifted * jax.nn.sigmoid(lifted) * value).astype(jnp.bfloat16)
        total = total + matmul(inner, transition_down[offset : offset + 256, :])
    result_ref[...] = (after + total.astype(jnp.bfloat16).astype(jnp.float32)).astype(jnp.bfloat16)

    for step in range(1, n_row):
        to_row(step).wait_send()
    for step in range(n_row):

        @pl.when(row_peer(step) != col)
        def _():
            for piece in pieces:
                to_owner(step, piece).wait_send()

    for step in range(1, n_col):
        for piece in pieces:
            to_col(step, piece).wait_send()
    for step in range(n_col):

        @pl.when(col_peer(step) != row)
        def _():
            for piece in pieces:
                to_row_owner(step, piece).wait_send()


def local_kernel(n_row, n_col, pair, residue_count, *rest):
    size, _, channels = pair.shape
    tokens = size * size
    rest = [leaf[None, :] if leaf.ndim == 1 else leaf for leaf in rest]
    operands = [pair.reshape(tokens, channels)] + rest
    vmem = pl.BlockSpec(memory_space=pltpu.VMEM)
    hbm = pl.BlockSpec(memory_space=pltpu.HBM)
    narrow = pltpu.VMEM((4, tokens, channels), jnp.bfloat16)
    wide = pltpu.VMEM((tokens, channels), jnp.float32)
    result = pl.pallas_call(
        functools.partial(block_kernel, size, n_row, n_col),
        out_shape=jax.ShapeDtypeStruct((tokens, channels), jnp.bfloat16),
        in_specs=[pl.BlockSpec(memory_space=pltpu.SMEM)] + [hbm] * len(operands),
        out_specs=vmem,
        scratch_shapes=[pltpu.VMEM(leaf.shape, leaf.dtype) for leaf in operands]
        + [wide] * 4
        + [narrow] * 6
        + [pltpu.SemaphoreType.DMA((4,))] * 2
        + [pltpu.SemaphoreType.DMA((4, size // 8))] * 6
        + [pltpu.SemaphoreType.DMA((len(operands),))],
        compiler_params=pltpu.CompilerParams(
            collective_id=0, has_side_effects=True, vmem_limit_bytes=62 * 1024 * 1024
        ),
    )(residue_count, *operands)
    return result.reshape(size, size, channels)


def local(pair, residue_count, *rest, n_row, n_col):
    hidden = rest[1].shape[1] // 4
    fits = n_row == 4 and n_col == 4 and pair.shape[0] == pair.shape[1]
    fits = fits and pair.shape[0] % 8 == 0 and pair.shape[0] <= 32
    if fits and hidden == pair.shape[2] and hidden % 128 == 0:
        return local_kernel(n_row, n_col, pair, residue_count, *rest)
    return local_plain(pair, residue_count, *rest)


def solution(mesh):
    placed = (
        P(("parts", "row"), "col", None),
        P("parts"),
        P(),
        P(),
        P(),
        P(),
        P(),
        P(),
        P(),
        P(),
        P(),
        P(),
        P(),
        P(),
        P(),
    )
    return jax.shard_map(
        functools.partial(
            local, n_row=mesh.shape["row"], n_col=mesh.shape["col"]
        ),
        mesh=mesh,
        in_specs=placed,
        out_specs=P(("parts", "row"), "col", None),
        check_vma=False,
    )
```

```python
import functools

import jax
import jax.numpy as jnp
from jax import lax
from jax.experimental import pallas as pl
from jax.experimental.pallas import tpu as pltpu
from jax.sharding import PartitionSpec as P

MESH = pl.DeviceIdType.MESH


def layer_norm(values, gain, axis):
    mean = jnp.mean(values, axis=axis, keepdims=True)
    centred = values - mean
    spread = jnp.mean(centred * centred, axis=axis, keepdims=True)
    return centred * lax.rsqrt(spread + 1e-05) * gain


def project(current, norm_gain, proj_w, gate_w, mask, form):
    normed = layer_norm(current.astype(jnp.float32), norm_gain, -1).astype(jnp.bfloat16)
    hidden = proj_w.shape[1] // 4
    left_part = jnp.einsum(
        form, normed, proj_w[:, : 2 * hidden], preferred_element_type=jnp.float32
    )
    left = (mask * jax.nn.sigmoid(left_part[:hidden]) * left_part[hidden:]).astype(jnp.bfloat16)
    right_part = jnp.einsum(
        form, normed, proj_w[:, 2 * hidden :], preferred_element_type=jnp.float32
    )
    right = (mask * jax.nn.sigmoid(right_part[:hidden]) * right_part[hidden:]).astype(jnp.bfloat16)
    gate = jnp.einsum("ijc,cd->ijd", normed, gate_w, preferred_element_type=jnp.float32)
    return (left, right, gate)


def finish(current, mixed, mix_gain, final_w, gate, form):
    mixnormed = layer_norm(mixed.astype(jnp.float32), mix_gain[:, None, None], 0).astype(
        jnp.bfloat16
    )
    change = jnp.einsum(form, mixnormed, final_w, preferred_element_type=jnp.float32)
    return (current.astype(jnp.float32) + jax.nn.sigmoid(gate) * change).astype(jnp.bfloat16)


def mix_over_col(left, right, incoming):
    left_wide, right_wide = (
        lax.all_to_all(left, "col", split_axis=0, concat_axis=2, tiled=True),
        lax.all_to_all(right, "col", split_axis=0, concat_axis=2, tiled=True),
    )
    if incoming:
        left_swapped = lax.all_to_all(left_wide, "row", split_axis=2, concat_axis=1, tiled=True)
        mixed = jnp.einsum(
            "hki,hkj->hij",
            left_swapped,
            lax.all_gather(right_wide, "row", axis=1, tiled=True),
            preferred_element_type=jnp.float32,
        )
    else:
        mixed = jnp.einsum(
            "hik,hjk->hij",
            left_wide,
            lax.all_gather(right_wide, "row", axis=1, tiled=True),
            preferred_element_type=jnp.float32,
        )
    return lax.all_to_all(
        mixed.astype(jnp.bfloat16), "col", split_axis=2, concat_axis=0, tiled=True
    )


def triangle(current, norm_gain, proj_w, gate_w, mix_gain, final_w, mask, incoming):
    left, right, gate = project(current, norm_gain, proj_w, gate_w, mask, "ijc,cf->fij")
    mixed = mix_over_col(left, right, incoming)
    return finish(current, mixed, mix_gain, final_w, gate, "hij,hc->ijc")


def local_plain(
    pair,
    residue_count,
    out_norm,
    out_proj,
    out_gate,
    out_mix_norm,
    out_final,
    inc_norm,
    inc_proj,
    inc_gate,
    inc_mix_norm,
    inc_final,
    transition_norm,
    transition_up,
    transition_down,
):
    tile_rows = pair.shape[0]
    tile_cols = pair.shape[1]
    row_place = lax.axis_index("row") * tile_rows + jnp.arange(tile_rows, dtype=jnp.int32)
    col_place = lax.axis_index("col") * tile_cols + jnp.arange(tile_cols, dtype=jnp.int32)
    valid_rows = (row_place < residue_count[0]).astype(jnp.float32)
    valid_cols = (col_place < residue_count[0]).astype(jnp.float32)
    mask = valid_rows[:, None] * valid_cols[None, :]
    after_one = triangle(pair, out_norm, out_proj, out_gate, out_mix_norm, out_final, mask, False)
    after_two = triangle(
        after_one, inc_norm, inc_proj, inc_gate, inc_mix_norm, inc_final, mask, True
    )
    normed = layer_norm(after_two.astype(jnp.float32), transition_norm, -1).astype(jnp.bfloat16)
    width = transition_down.shape[0]
    total = jnp.zeros(after_two.shape, jnp.float32)
    for offset in range(0, width, 128):
        gate_part = jnp.einsum(
            "ijc,cf->ijf",
            normed,
            transition_up[:, offset : offset + 128],
            preferred_element_type=jnp.float32,
        )
        value_part = jnp.einsum(
            "ijc,cf->ijf",
            normed,
            transition_up[:, width + offset : width + offset + 128],
            preferred_element_type=jnp.float32,
        )
        inner = (jax.nn.silu(gate_part) * value_part).astype(jnp.bfloat16)
        total = total + jnp.einsum(
            "ijf,fc->ijc",
            inner,
            transition_down[offset : offset + 128],
            preferred_element_type=jnp.float32,
        )
    return (after_two.astype(jnp.float32) + total).astype(jnp.bfloat16)


def norm_rows(values, gain):
    mean = jnp.mean(values, axis=-1, keepdims=True)
    centred = values - mean
    spread = jnp.mean(centred * centred, axis=-1, keepdims=True)
    return centred * lax.rsqrt(spread + 1e-05) * gain


def matmul(left, right):
    return jnp.dot(left, right, preferred_element_type=jnp.float32)


def masked_half(normed, proj_ref, start, hidden, mask):
    part = matmul(normed, proj_ref[:, start : start + 2 * hidden])
    return (mask * jax.nn.sigmoid(part[:, :hidden]) * part[:, hidden:]).astype(jnp.bfloat16)


def contract(size, left_ref, right_ref, out_ref, out_slot, piece):
    def step(k, totals):
        block = right_ref[pl.ds(pl.multiple_of(k * size, 8), size), :]
        base = pl.multiple_of((piece * size + k) * 8, 8)
        return tuple(
            total + left_ref[pl.ds(base + place, 1), :] * block
            for place, total in enumerate(totals)
        )

    zero = jnp.zeros((size, right_ref.shape[1]), jnp.float32)
    totals = lax.fori_loop(0, size, step, (zero,) * 8, unroll=6)
    out_ref[out_slot, piece * 8 * size : (piece + 1) * 8 * size, :] = jnp.concatenate(
        totals, axis=0
    ).astype(jnp.bfloat16)


def by_pieces(size, values, out_ref):
    for k in range(size):
        for piece in range(size // 8):
            source = k * size + piece * 8
            target = (piece * size + k) * 8
            out_ref[target : target + 8, :] = values[source : source + 8, :]


def block_kernel(
    size,
    n_row,
    n_col,
    count_ref,
    *refs,
):
    sources, result_ref, held, refs = refs[:14], refs[14], refs[15:29], refs[29:]
    (
        pair_ref,
        out_norm,
        out_proj,
        out_gate,
        out_mix_norm,
        out_final,
        inc_norm,
        inc_proj,
        inc_gate,
        inc_mix_norm,
        inc_final,
        transition_norm,
        transition_up,
        transition_down,
    ) = held
    (
        turn_a,
        turn_b,
        wide_left,
        wide_right,
        right_in,
        part_out,
        part_in,
        left_in,
        sum_out,
        sum_in,
        send_a,
        recv_a,
        send_b,
        recv_b,
        send_c,
        recv_c,
        send_d,
        recv_d,
        load,
    ) = refs
    row = lax.axis_index("row")
    col = lax.axis_index("col")
    tokens = size * size
    pieces = range(size // 8)
    hidden = out_proj.shape[1] // 4

    loads = [
        pltpu.make_async_copy(source, target, load.at[place])
        for place, (source, target) in enumerate(zip(sources, held))
    ]
    for one in loads:
        one.start()

    def row_peer(step):
        place = (row // 2 + step // 2) % (n_row // 2)
        return place * 2 + (row % 2 + step % 2) % 2

    def col_peer(step):
        return (col + step) % n_col

    barrier = pltpu.get_barrier_semaphore()
    for step in range(1, n_row):
        pl.semaphore_signal(
            barrier, inc=1, device_id={"row": row_peer(step)}, device_id_type=MESH
        )
    for step in range(1, n_col):
        pl.semaphore_signal(
            barrier, inc=1, device_id={"col": col_peer(step)}, device_id_type=MESH
        )

    def copy(source, target, send, recv, where):
        return pltpu.make_async_remote_copy(
            src_ref=source,
            dst_ref=target,
            send_sem=send,
            recv_sem=recv,
            device_id=where,
            device_id_type=MESH,
        )

    def to_row(step):
        hop = 1 if step == 3 else step
        return copy(
            right_in.at[step - hop], right_in.at[step], send_a.at[step], recv_a.at[step],
            {"row": row_peer(hop)},
        )

    def to_owner(step, piece):
        part = pl.ds(piece * 8 * size, 8 * size)
        return copy(
            part_out.at[step, part], part_in.at[col, part], send_b.at[step, piece], recv_b.at[col, piece],
            {"col": row_peer(step)},
        )

    def from_col(sender, piece):
        part = pl.ds(piece * 8 * size, 8 * size)
        return copy(
            part_out.at[0, part], part_in.at[sender, part], send_b.at[0, piece], recv_b.at[sender, piece],
            {"col": sender},
        )

    def to_col(step, piece):
        part = pl.ds(piece * 8 * size, 8 * size)
        return copy(
            left_in.at[col, part], left_in.at[col, part], send_c.at[step, piece], recv_c.at[col, piece],
            {"col": col_peer(step)},
        )

    def left_from(sender, piece):
        part = pl.ds(piece * 8 * size, 8 * size)
        return copy(
            left_in.at[col, part], left_in.at[sender, part], send_c.at[0, piece], recv_c.at[sender, piece],
            {"col": sender},
        )

    def to_row_owner(step, piece):
        part = pl.ds(piece * 8 * size, 8 * size)
        return copy(
            sum_out.at[step, part], sum_in.at[row, part], send_d.at[step, piece], recv_d.at[row, piece],
            {"row": col_peer(step)},
        )

    def from_row(sender, piece):
        part = pl.ds(piece * 8 * size, 8 * size)
        return copy(
            sum_out.at[0, part], sum_in.at[sender, part], send_d.at[0, piece], recv_d.at[sender, piece],
            {"row": sender},
        )

    shape = (size, size, hidden)
    first = lax.broadcasted_iota(jnp.int32, shape, 0)
    second = lax.broadcasted_iota(jnp.int32, shape, 1)
    count = count_ref[0]

    def mask_of(a, b):
        real = jnp.logical_and(a < count, b < count)
        return jnp.where(real, 1.0, 0.0).astype(jnp.float32).reshape(tokens, hidden)

    mask = mask_of(first + row * size, second + col * size)
    mask_turned = mask_of(first + col * size, second + row * size)

    for one in loads[:3]:
        one.wait()
    normed = norm_rows(pair_ref[...].astype(jnp.float32), out_norm[...])
    turn_a[...] = normed
    for k in range(size):
        turn_b[k * size : (k + 1) * size, :] = turn_a[pl.ds(k, size, stride=size), :]
    turned = turn_b[...].astype(jnp.bfloat16)
    right_in[0] = masked_half(turned, out_proj, 2 * hidden, hidden, mask_turned)
    pl.semaphore_wait(barrier, n_row + n_col - 2)
    for step in (2, 1):
        to_row(step).start()
    left = masked_half(turned, out_proj, 0, hidden, mask_turned)
    by_pieces(size, left.astype(jnp.float32), wide_left)
    for step in range(n_row):
        if step > 0:
            to_row(step).wait_recv()
        if step == 2:
            to_row(3).start()
        wide_right[...] = right_in[step].astype(jnp.float32)
        for piece in pieces:
            contract(size, wide_left, wide_right, part_out, step, piece)

            @pl.when(row_peer(step) != col)
            def _():
                to_owner(step, piece).start()

        @pl.when(row_peer(step) == col)
        def _():
            part_in[col] = part_out[step]

    for one in loads[3:6]:
        one.wait()
    gate = jax.nn.sigmoid(matmul(normed.astype(jnp.bfloat16), out_gate[...]))
    for sender in range(n_col):

        @pl.when(sender != col)
        def _():
            for piece in pieces:
                from_col(sender, piece).wait_recv()

    mixed = part_in[0].astype(jnp.float32)
    for sender in range(1, n_col):
        mixed = mixed + part_in[sender].astype(jnp.float32)
    mixed = norm_rows(mixed.astype(jnp.bfloat16).astype(jnp.float32), out_mix_norm[...])
    change = matmul(mixed.astype(jnp.bfloat16), out_final[...])
    after = (pair_ref[...].astype(jnp.float32) + gate * change).astype(jnp.bfloat16)
    after = after.astype(jnp.float32)

    for one in loads[6:]:
        one.wait()
    normed = norm_rows(after, inc_norm[...]).astype(jnp.bfloat16)
    left = masked_half(normed, inc_proj, 0, hidden, mask)
    by_pieces(size, left.astype(jnp.float32), wide_left)
    left_in[col] = wide_left[...].astype(jnp.bfloat16)
    for piece in pieces:
        for step in (1, 3, 2):
            to_col(step, piece).start()
    wide_right[...] = masked_half(normed, inc_proj, 2 * hidden, hidden, mask).astype(jnp.float32)
    gate = jax.nn.sigmoid(matmul(normed, inc_gate[...]))
    turn_a[...] = after
    turn_b[...] = gate
    order = [(0, piece) for piece in pieces]
    order += [(step, piece) for piece in pieces for step in (1, 3, 2)]
    for step, piece in order:
        owner = col_peer(step)
        if step > 0:
            left_from(owner, piece).wait_recv()
            part = pl.ds(piece * 8 * size, 8 * size)
            wide_left[part, :] = left_in[owner, part, :].astype(jnp.float32)
        contract(size, wide_left, wide_right, sum_out, step, piece)

        @pl.when(owner != row)
        def _():
            to_row_owner(step, piece).start()

        @pl.when(owner == row)
        def _():
            part = pl.ds(piece * 8 * size, 8 * size)
            sum_in[row, part, :] = sum_out[step, part, :]

    for sender in range(n_row):

        @pl.when(sender != row)
        def _():
            for piece in pieces:
                from_row(sender, piece).wait_recv()

    mixed = sum_in[0].astype(jnp.float32)
    for sender in range(1, n_row):
        mixed = mixed + sum_in[sender].astype(jnp.float32)
    mixed = norm_rows(mixed.astype(jnp.bfloat16).astype(jnp.float32), inc_mix_norm[...])
    change = matmul(mixed.astype(jnp.bfloat16), inc_final[...])
    after = (turn_a[...] + turn_b[...] * change).astype(jnp.bfloat16).astype(jnp.float32)

    normed = norm_rows(after, transition_norm[...]).astype(jnp.bfloat16)
    width = transition_down.shape[0]
    total = jnp.zeros((tokens, hidden), jnp.float32)
    for offset in range(0, width, 256):
        lifted = matmul(normed, transition_up[:, offset : offset + 256])
        value = matmul(normed, transition_up[:, width + offset : width + offset + 256])
        inner = (lifted * jax.nn.sigmoid(lifted) * value).astype(jnp.bfloat16)
        total = total + matmul(inner, transition_down[offset : offset + 256, :])
    result_ref[...] = (after + total.astype(jnp.bfloat16).astype(jnp.float32)).astype(jnp.bfloat16)

    for step in range(1, n_row):
        to_row(step).wait_send()
    for step in range(n_row):

        @pl.when(row_peer(step) != col)
        def _():
            for piece in pieces:
                to_owner(step, piece).wait_send()

    for step in range(1, n_col):
        for piece in pieces:
            to_col(step, piece).wait_send()
    for step in range(n_col):

        @pl.when(col_peer(step) != row)
        def _():
            for piece in pieces:
                to_row_owner(step, piece).wait_send()


def local_kernel(n_row, n_col, pair, residue_count, *rest):
    size, _, channels = pair.shape
    tokens = size * size
    rest = [leaf[None, :] if leaf.ndim == 1 else leaf for leaf in rest]
    operands = [pair.reshape(tokens, channels)] + rest
    vmem = pl.BlockSpec(memory_space=pltpu.VMEM)
    hbm = pl.BlockSpec(memory_space=pltpu.HBM)
    narrow = pltpu.VMEM((4, tokens, channels), jnp.bfloat16)
    wide = pltpu.VMEM((tokens, channels), jnp.float32)
    result = pl.pallas_call(
        functools.partial(block_kernel, size, n_row, n_col),
        out_shape=jax.ShapeDtypeStruct((tokens, channels), jnp.bfloat16),
        in_specs=[pl.BlockSpec(memory_space=pltpu.SMEM)] + [hbm] * len(operands),
        out_specs=vmem,
        scratch_shapes=[pltpu.VMEM(leaf.shape, leaf.dtype) for leaf in operands]
        + [wide] * 4
        + [narrow] * 6
        + [pltpu.SemaphoreType.DMA((4,))] * 2
        + [pltpu.SemaphoreType.DMA((4, size // 8))] * 6
        + [pltpu.SemaphoreType.DMA((len(operands),))],
        compiler_params=pltpu.CompilerParams(
            collective_id=0, has_side_effects=True, vmem_limit_bytes=62 * 1024 * 1024
        ),
    )(residue_count, *operands)
    return result.reshape(size, size, channels)


def local(pair, residue_count, *rest, n_row, n_col):
    hidden = rest[1].shape[1] // 4
    fits = n_row == 4 and n_col == 4 and pair.shape[0] == pair.shape[1]
    fits = fits and pair.shape[0] % 8 == 0 and pair.shape[0] <= 32
    if fits and hidden == pair.shape[2] and hidden % 128 == 0:
        return local_kernel(n_row, n_col, pair, residue_count, *rest)
    return local_plain(pair, residue_count, *rest)


def solution(mesh):
    placed = (
        P(("parts", "row"), "col", None),
        P("parts"),
        P(),
        P(),
        P(),
        P(),
        P(),
        P(),
        P(),
        P(),
        P(),
        P(),
        P(),
        P(),
        P(),
    )
    return jax.shard_map(
        functools.partial(
            local, n_row=mesh.shape["row"], n_col=mesh.shape["col"]
        ),
        mesh=mesh,
        in_specs=placed,
        out_specs=P(("parts", "row"), "col", None),
        check_vma=False,
    )
```
